512 devices in a mesh: eig: 32 (over z_lo, x, core), tok: 16 (over y, z_hi).
Axes of the slice: x: 4, y: 4, z: 16 (z_hi: 4, z_lo: 4; z = z_hi * 4 + z_lo), core: 2. Of those that a mesh axis runs over, the one named last changes fastest.
Arguments:
- query_grad: float32 [7168, 2048], P('eig', 'tok'), may hold values from -6 to 6
- basis_in: float32 [2048, 2048], P('tok', 'eig'), may hold values from -0.125 to 0.125
- basis_out: float32 [7168, 7168], P('eig', 'tok'), may hold values from -0.0625 to 0.0625
- spectrum: float32 [7168, 2048], P('tok', 'eig'), may hold values from 0.02 to 20
- activations: float32 [4096, 2048], P('tok', 'eig'), may hold values from -0.125 to 0.125
- out_grads: float32 [4096, 7168], P('tok', 'eig'), may hold values from -0.0625 to 0.0625
Outputs:
- influence: float32 [4096], P('tok')
The draws below stay inside these ranges and needn't reach their ends.
All inputs are finite; a program needn't handle non-finite values.
Results may differ from the reference program's by a relative error of at most 0.000094.
Values sent between devices are 32-bit elements; how exact they have to be, the bound alone decides.
A program may use at most 64 MiB of HBM per device.

```python
import math
import jax
import jax.numpy as jnp
from jax import lax

D = 2048
FF = 7168
TOKENS = 4096


def shard_levels(stream_key, extent, pieces, least, top_value):
    factor_of, own = 1.0, jax.random.fold_in(stream_key, 6)
    for position, shards_of in pieces:
        heights = jnp.exp(jax.random.uniform(jax.random.fold_in(own, position), (shards_of,), jnp.float32, least / len(pieces), top_value / len(pieces)))
        factor_of = factor_of * jnp.repeat(heights, extent[position] // shards_of).reshape([-1 if axis == position else 1 for axis in range(len(extent))])
    return factor_of


def noise(key, shape, deviation, reach, split=(), kind=jnp.bfloat16):
    drawn = jax.random.normal(key, shape, jnp.float32) * deviation
    if len(split) > 0:
        drawn = shard_levels(key, shape, split, -0.22, 0.18) * drawn
    return jnp.clip(drawn, min=-reach, max=reach).astype(kind)


def setup_inputs(seed: int = 0) -> dict:
    key_list = jax.random.split(jax.random.key(seed), 7)
    return {
        "query_grad": noise(key_list[0], (FF, D), 1.0, 6.0, ((0, 32), (1, 16)), jnp.float32),
        "basis_in": noise(key_list[1], (D, D), D ** -0.5, 0.125, ((0, 16), (1, 32)), jnp.float32),
        "basis_out": noise(key_list[2], (FF, FF), FF ** -0.5, 0.0625, ((0, 32), (1, 16)), jnp.float32),
        "spectrum": jnp.clip(jnp.exp(math.log(20.0) - 6.9077553 * jax.random.uniform(key_list[3], (FF, D), jnp.float32) ** shard_levels(key_list[3], (FF, D), ((0, 16), (1, 32)), -0.2, 0.2)), 0.02, 20.0),
        "activations": noise(key_list[4], (TOKENS, D), D ** -0.5, 0.125, ((0, 16), (1, 32)), jnp.float32),
        "out_grads": noise(key_list[5], (TOKENS, FF), FF ** -0.5, 0.0625, ((0, 16), (1, 32)), jnp.float32),
    }


damping = 0.1


def reference(query_grad, basis_in, basis_out, spectrum, activations, out_grads):
    highest = lax.Precision.HIGHEST
    rotated_in = jnp.dot(query_grad, basis_in, precision=highest, preferred_element_type=jnp.float32)
    rotated = jnp.dot(basis_out.T, rotated_in, precision=highest, preferred_element_type=jnp.float32)
    scaled = rotated / (spectrum + damping)
    back_out = jnp.dot(basis_out, scaled, precision=highest, preferred_element_type=jnp.float32)
    precond = jnp.dot(back_out, basis_in.T, precision=highest, preferred_element_type=jnp.float32)
    mapped = jnp.dot(activations, precond.T, precision=highest, preferred_element_type=jnp.float32)
    return jnp.sum(mapped * out_grads, axis=1)
```

```python
import jax
import jax.numpy as jnp
from jax import lax
from jax.experimental import pallas as pl
from jax.experimental.pallas import tpu as pltpu
from jax.sharding import PartitionSpec as P

damping = 0.1
MESH = pl.DeviceIdType.MESH
F32, BF16 = jnp.float32, jnp.bfloat16
SIZE = dict(zl=4, x=4, k=2, y=4, zh=4)
N_SEMS = 128


def coords():
    e, t = lax.axis_index("eig"), lax.axis_index("tok")
    return dict(zl=e // 8, x=(e // 2) % 4, k=e % 2, y=t // 4, zh=t % 4)


def place(c, **other):
    d = dict(c, **other)
    return (d["zl"] * 8 + d["x"] * 2 + d["k"], d["y"] * 4 + d["zh"])


def peer(c, axis, d):
    return place(c, **{axis: lax.rem(c[axis] + d, SIZE[axis])})


def at_distance(c, axis, d):
    return lax.rem(c[axis] + d, SIZE[axis])


def split(v):
    hi = v.astype(BF16)
    return hi, (v - hi.astype(F32)).astype(BF16)


def mm(left, right, dims=((1,), (0,))):
    return lax.dot_general(left, right, (dims, ((), ())), preferred_element_type=F32)


def dot3(lh, ll, cat, dims=((1,), (0,))):
    n = cat.shape[1] // 2
    wide = mm(lh, cat, dims)
    return wide[:, :n] + wide[:, n:] + mm(ll, cat[:, :n], dims)


def both(v):
    return jnp.concatenate(split(v), axis=1)


def kernel(
    g, b, o, sp, a, og, out,
    oA, oB, ohi, olo, gall, asw, bsw, spsw, ball, aA, aB, wall, ogA, ogB,
    tp, tk, ts, tz, tA, tB, sall, scat, bp, bz, f0, f1, f2, f3, f4, f5, f6,
    ss, rs, ls,
):
    c = coords()
    x, y, zl, zh, k = c["x"], c["y"], c["zl"], c["zh"], c["k"]
    used = [0]
    sent = []

    def remote(src, dst, device):
        i = used[0]
        used[0] += 1
        return pltpu.make_async_remote_copy(
            src_ref=src, dst_ref=dst, send_sem=ss.at[i], recv_sem=rs.at[i], device_id=device, device_id_type=MESH
        )

    def start(copies):
        for q in copies:
            q.start()
            sent.append(q)
        return copies

    def arrived(copies):
        for q in copies:
            q.wait_recv()

    class Maybe:
        def __init__(self, own, src, dst, device):
            self.own, self.far = own, remote(src, dst, device)
            self.near = pltpu.make_async_copy(src, dst, ls.at[used[0]])

        def start(self):
            pl.when(jnp.logical_not(self.own))(self.far.start)
            pl.when(self.own)(self.near.start)

        def wait_recv(self):
            pl.when(jnp.logical_not(self.own))(self.far.wait_recv)
            pl.when(self.own)(self.near.wait)

        def wait_send(self):
            pl.when(jnp.logical_not(self.own))(self.far.wait_send)

    swap_yz = dict(y=zl, zl=y)
    swap_xz = place(c, x=zh, zh=x)
    own_yz, own_xz = y == zl, x == zh

    barrier = pltpu.get_barrier_semaphore()
    for axis in ("x", "y", "zl", "zh", "k"):
        for d in range(1, SIZE[axis]):
            pl.semaphore_signal(barrier, inc=1, device_id=peer(c, axis, d), device_id_type=MESH)

    @pl.when(jnp.logical_not(own_yz))
    def _():
        pl.semaphore_signal(barrier, inc=1, device_id=place(c, **swap_yz), device_id_type=MESH)
        pl.semaphore_signal(barrier, inc=1, device_id=place(c, k=1 - k, **swap_yz), device_id_type=MESH)

    @pl.when(jnp.logical_not(own_xz))
    def _():
        pl.semaphore_signal(barrier, inc=1, device_id=swap_xz, device_id_type=MESH)

    own = [
        pltpu.make_async_copy(o.at[pl.ds(0, 112)], oA.at[y, x], ls.at[0]),
        pltpu.make_async_copy(o.at[pl.ds(112, 112)], oB.at[x, y], ls.at[1]),
    ]
    used[0] = 2
    for q in own:
        q.start()
    pl.semaphore_wait(barrier, 16 - jnp.where(own_yz, 2, 0) - jnp.where(own_xz, 1, 0))

    def gather_first(bufA, bufB, srcA=None, srcB=None):
        srcA = bufA.at[y, x] if srcA is None else srcA
        srcB = bufB.at[x, y] if srcB is None else srcB
        la = [remote(srcA, bufA.at[y, x], peer(c, "x", d)) for d in (1, 3, 2)]
        lb = [remote(srcB, bufB.at[x, y], peer(c, "y", d)) for d in (1, 3, 2)]
        return start(la), start(lb)

    def gather_second(bufA, bufB, first):
        arrived(first[0])
        la = start([remote(bufA.at[y], bufA.at[y], peer(c, "y", d)) for d in (1, 3, 2)])
        arrived(first[1])
        lb = start([remote(bufB.at[x], bufB.at[x], peer(c, "x", d)) for d in (1, 3, 2)])
        return la + lb

    qg = start([Maybe(own_xz, g, gall.at[x], swap_xz)])
    o1 = gather_first(oA, oB, o.at[pl.ds(0, 112)], o.at[pl.ds(112, 112)])
    qb, qa, qs = [], [], []
    for list_, src, dst, rows in ((qb, b, bsw, 64), (qa, a, asw, 128), (qs, sp, spsw, 224)):
        list_.append(Maybe(own_yz, src.at[pl.ds(pl.multiple_of(k * rows, rows), rows)], dst.at[k], place(c, **swap_yz)))
        list_.append(
            remote(src.at[pl.ds(pl.multiple_of((1 - k) * rows, rows), rows)], dst.at[k], place(c, k=1 - k, **swap_yz))
        )
        start(list_)
    qog = start([
        Maybe(own_xz, og.at[pl.ds(0, 128)], ogA.at[y, zh], swap_xz),
        Maybe(own_xz, og.at[pl.ds(128, 128)], ogB.at[zh, y], swap_xz),
    ])

    arrived(qg)
    g2 = start([remote(gall.at[zh], gall.at[zh], peer(c, "zh", d)) for d in (1, 3, 2)])

    arrived(qb)
    ball[zl, zh, k] = jnp.concatenate([bsw[0], bsw[1]], axis=1)
    b2 = start([remote(ball.at[zl, zh, k], ball.at[zl, zh, k], peer(c, "zh", d)) for d in (1, 3, 2)])

    for q in own:
        q.wait()
    o2 = gather_second(oA, oB, o1)

    arrived(qa)
    av = jnp.concatenate([asw[0], asw[1]], axis=1)
    aA[y, x] = av[:64]
    aB[x, y] = av[64:]
    a1 = gather_first(aA, aB)

    arrived(b2)
    b3 = start([remote(ball.at[zl, :, k], ball.at[zl, :, k], peer(c, "zl", d)) for d in (1, 3, 2)])
    a2 = gather_second(aA, aB, a1)
    arrived(b3)
    b4 = start([remote(ball.at[:, :, k], ball.at[:, :, k], peer(c, "k", 1))])

    arrived(g2)
    gcat = both(gall[...].reshape(896, 128))
    arrived(o2)

    def t_step(i, _):
        for j in range(4):
            for half, block in ((0, oA[i, j]), (1, oB[j, i])):
                hi, lo = split(block)
                ohi[i, j, half * 112 : half * 112 + 112] = hi
                olo[i, j, half * 112 : half * 112 + 112] = lo
        part = dot3(ohi[i].reshape(896, 448), olo[i].reshape(896, 448), gcat, ((0,), (0,)))
        tp[0, i] = part[:224]
        tp[1, i] = part[224:]
        return 0

    lax.fori_loop(0, 4, t_step, 0)
    t1 = start([remote(tp.at[1 - k], tk, peer(c, "k", 1))])

    arrived(a2)
    arrived(b4)
    bcat = both(ball[...].reshape(2048, 128))
    blocks = [(i, j) for i in range(4) for j in range(4)]
    arows = jnp.concatenate(
        [
            jnp.concatenate([aA[i, j] for i, j in blocks], axis=1),
            jnp.concatenate([aB[j, i] for i, j in blocks], axis=1),
        ],
        axis=0,
    )
    wall[zl, zh, k] = dot3(*split(arows), bcat)

    arrived(t1)
    ts[...] = tp[k] + tk[...]
    t2 = start([remote(ts.at[at_distance(c, "zl", d)], tz.at[d], peer(c, "zl", d)) for d in (1, 3, 2)])
    w1 = start([remote(wall.at[zl, zh, k], wall.at[zl, zh, k], peer(c, "zh", d)) for d in (1, 3, 2)])
    arrived(t2)
    tv = ts[zl] + tz[1] + tz[2] + tz[3]
    tA[y, x] = tv[:112]
    tB[x, y] = tv[112:]
    t3 = gather_first(tA, tB)
    t4 = gather_second(tA, tB, t3)
    arrived(qog)
    og1 = gather_first(ogA, ogB)
    arrived(w1)
    w2 = start([remote(wall.at[zl, :, k], wall.at[zl, :, k], peer(c, "zl", d)) for d in (1, 3, 2)])
    arrived(qs)
    spv = jnp.concatenate([spsw[0], spsw[1]], axis=1) + damping
    arrived(t4)

    trows = jnp.concatenate(
        [
            jnp.concatenate([tA[i, j] for i, j in blocks], axis=1),
            jnp.concatenate([tB[j, i] for i, j in blocks], axis=1),
        ],
        axis=0,
    )
    bcat = both(ball[...].reshape(2048, 128))
    sall[zl, k] = dot3(*split(trows), bcat) / spv
    s1 = start([remote(sall.at[zl, k], sall.at[zl, k], peer(c, "zl", d)) for d in (1, 3, 2)])
    s2 = start([remote(sall.at[zl, k], sall.at[zl, k], peer(c, "k", 1))])
    for q, d in zip(s1, (1, 3, 2)):
        q.wait_recv()
        origin = lax.rem(zl - d + 4, 4)
        s2 += start([remote(sall.at[origin, k], sall.at[origin, k], peer(c, "k", 1))])
    og2 = gather_second(ogA, ogB, og1)
    arrived(w2)
    w3 = start([remote(wall.at[:, :, k], wall.at[:, :, k], peer(c, "k", 1))])
    arrived(s2)

    scat[...] = both(sall[...].reshape(1792, 128)).reshape(4, 448, 256)

    def b_step(j, _):
        total = dot3(ohi[0, j], olo[0, j], scat[0])
        for i in range(1, 4):
            total = total + dot3(ohi[i, j], olo[i, j], scat[i])
        bp[j] = total
        return 0

    lax.fori_loop(0, 4, b_step, 0)
    k1 = start([remote(bp.at[at_distance(c, "zh", d)], bz.at[d], peer(c, "zh", d)) for d in (1, 3, 2)])
    arrived(og2)
    arrived(w3)
    arrived(k1)
    kcat = both(bp[zh] + bz[1] + bz[2] + bz[3])

    def f_step(n, _):
        i, j = n // 4, n % 4
        rows = jnp.concatenate([ogA[i, j], ogB[j, i]], axis=0)
        v = dot3(*split(rows), kcat) * wall[i, j].reshape(256, 128)
        f0[i, j] = jnp.sum(v.T.reshape(16, 8, 256), axis=0)
        return 0

    lax.fori_loop(0, 16, f_step, 0)
    arrived(start([remote(f0.at[at_distance(c, "y", d)], f1.at[d], peer(c, "y", d)) for d in (1, 3, 2)]))
    f2[...] = f0[y] + f1[1] + f1[2] + f1[3]
    arrived(start([remote(f2.at[at_distance(c, "zh", d)], f3.at[d], peer(c, "zh", d)) for d in (1, 3, 2)]))
    f4[x] = f2[zh] + f3[1] + f3[2] + f3[3]
    arrived(start([remote(f4.at[x], f4.at[x], peer(c, "x", d)) for d in (1, 3, 2)]))
    f5[zl] = f4[0] + f4[1] + f4[2] + f4[3]
    arrived(start([remote(f5.at[zl], f5.at[zl], peer(c, "zl", d)) for d in (1, 3, 2)]))
    f6[k] = f5[0] + f5[1] + f5[2] + f5[3]
    arrived(start([remote(f6.at[k], f6.at[k], peer(c, "k", 1))]))
    out[...] = jnp.sum(f6[0] + f6[1], axis=0, keepdims=True)
    for q in sent:
        q.wait_send()


def body(query_grad, basis_in, basis_out, spectrum, activations, out_grads):
    def vmem(*shape, dtype=F32):
        return pltpu.VMEM(shape, dtype)

    out = pl.pallas_call(
        kernel,
        out_shape=jax.ShapeDtypeStruct((1, 256), F32),
        in_specs=[pl.BlockSpec(memory_space=pl.ANY)] * 6,
        out_specs=pl.BlockSpec(memory_space=pltpu.VMEM),
        scratch_shapes=[
            vmem(4, 4, 112, 448),
            vmem(4, 4, 112, 448),
            vmem(4, 4, 224, 448, dtype=BF16),
            vmem(4, 4, 224, 448, dtype=BF16),
            vmem(4, 224, 128),
            vmem(2, 128, 64),
            vmem(2, 64, 64),
            vmem(2, 224, 64),
            vmem(4, 4, 2, 64, 128),
            vmem(4, 4, 64, 128),
            vmem(4, 4, 64, 128),
            vmem(4, 4, 2, 128, 128),
            vmem(4, 4, 128, 224),
            vmem(4, 4, 128, 224),
            vmem(2, 4, 224, 128),
            vmem(4, 224, 128),
            vmem(4, 224, 128),
            vmem(4, 224, 128),
            vmem(4, 4, 112, 128),
            vmem(4, 4, 112, 128),
            vmem(4, 2, 224, 128),
            vmem(4, 448, 256, dtype=BF16),
            vmem(4, 224, 128),
            vmem(4, 224, 128),
            vmem(4, 4, 8, 256),
            vmem(4, 4, 8, 256),
            vmem(4, 8, 256),
            vmem(4, 8, 256),
            vmem(4, 8, 256),
            vmem(4, 8, 256),
            vmem(2, 8, 256),
            pltpu.SemaphoreType.DMA((N_SEMS,)),
            pltpu.SemaphoreType.DMA((N_SEMS,)),
            pltpu.SemaphoreType.DMA((N_SEMS,)),
        ],
        compiler_params=pltpu.CompilerParams(
            collective_id=0, has_side_effects=True, vmem_limit_bytes=56 * 1024 * 1024
        ),
    )(query_grad, basis_in, basis_out, spectrum, activations, out_grads)
    return out.reshape(256)


def solution(mesh):
    in_specs = (
        P("eig", "tok"),
        P("tok", "eig"),
        P("eig", "tok"),
        P("tok", "eig"),
        P("tok", "eig"),
        P("tok", "eig"),
    )
    out_specs = P("tok")
    return jax.shard_map(body, mesh=mesh, in_specs=in_specs, out_specs=out_specs, check_vma=False)
```

```python
import jax
import jax.numpy as jnp
from jax import lax
from jax.experimental import pallas as pl
from jax.experimental.pallas import tpu as pltpu
from jax.sharding import PartitionSpec as P

damping = 0.1
MESH = pl.DeviceIdType.MESH
F32, BF16 = jnp.float32, jnp.bfloat16
SIZE = dict(zl=4, x=4, k=2, y=4, zh=4)
N_SEMS = 256
ORDER = (1, 3, 2)


def coords():
    e, t = lax.axis_index("eig"), lax.axis_index("tok")
    return dict(zl=e // 8, x=(e // 2) % 4, k=e % 2, y=t // 4, zh=t % 4)


def place(c, **other):
    d = dict(c, **other)
    return (d["zl"] * 8 + d["x"] * 2 + d["k"], d["y"] * 4 + d["zh"])


def peer(c, axis, d):
    return place(c, **{axis: lax.rem(c[axis] + d, SIZE[axis])})


def at_distance(c, axis, d):
    return lax.rem(c[axis] + d, SIZE[axis])


def split(v):
    hi = v.astype(BF16)
    return hi, (v - hi.astype(F32)).astype(BF16)


def mm(left, right, dims=((1,), (0,))):
    return lax.dot_general(left, right, (dims, ((), ())), preferred_element_type=F32)


def dot3(lh, ll, cat, dims=((1,), (0,))):
    n = cat.shape[1] // 2
    wide = mm(lh, cat, dims)
    return wide[:, :n] + wide[:, n:] + mm(ll, cat[:, :n], dims)


def both(v, axis):
    return jnp.concatenate(split(v), axis=axis)


def kernel(
    g, bt, o, spt, at, ogt, out,
    oA, oB, ohi, olo, gz, gall, spsw, damped, ball, bcat, aAB, wall, wcat, ogAB,
    tp, tk, ts, tz, tA, tB, sall, scat, bp, bz, f0, f1, f2, f3, f4, f5,
    ss, rs, ls,
):
    c = coords()
    x, y, zl, zh, k = c["x"], c["y"], c["zl"], c["zh"], c["k"]
    used = [0]
    sent = []

    def remote(src, dst, device):
        i = used[0]
        used[0] += 1
        return pltpu.make_async_remote_copy(
            src_ref=src, dst_ref=dst, send_sem=ss.at[i], recv_sem=rs.at[i], device_id=device, device_id_type=MESH
        )

    def start(copies):
        for q in copies:
            q.start()
            sent.append(q)
        return copies

    def arrived(copies):
        for q in copies:
            q.wait_recv()

    class Maybe:
        def __init__(self, own, src, dst, device):
            self.own, self.far = own, remote(src, dst, device)
            self.near = pltpu.make_async_copy(src, dst, ls.at[used[0]])

        def start(self):
            pl.when(jnp.logical_not(self.own))(self.far.start)
            pl.when(self.own)(self.near.start)

        def wait_recv(self):
            pl.when(jnp.logical_not(self.own))(self.far.wait_recv)
            pl.when(self.own)(self.near.wait)

        def wait_send(self):
            pl.when(jnp.logical_not(self.own))(self.far.wait_send)

    def to_peers(axis, src, dst):
        return start([remote(src, dst, peer(c, axis, d)) for d in ORDER])

    def scatter(axis, src, dst):
        return start([remote(src.at[at_distance(c, axis, d)], dst.at[d], peer(c, axis, d)) for d in ORDER])

    def summed(own, got):
        return own + got[1] + got[2] + got[3]

    swap_yz = place(c, y=zl, zl=y)
    swap_yz_far = place(c, y=zl, zl=y, k=1 - k)
    own_yz = y == zl
    plane = [
        place(c, x=at_distance(c, "x", i), y=at_distance(c, "y", j)) for i in range(4) for j in range(4) if i or j
    ]
    column = [
        place(c, zl=at_distance(c, "zl", i), zh=at_distance(c, "zh", j)) for i in range(4) for j in range(4) if i or j
    ]
    z = zh * 4 + zl

    def along_z(d):
        other = lax.rem(z + d, 16)
        return place(c, zl=other % 4, zh=other // 4)

    og_half = zh // 2
    og_slot = ogAB.at[og_half, y + og_half * (x - y), x + og_half * (y - x), zh % 2]

    own = [
        pltpu.make_async_copy(o.at[pl.ds(0, 112)], oA.at[y, x], ls.at[0]),
        pltpu.make_async_copy(o.at[pl.ds(112, 112)], oB.at[x, y], ls.at[1]),
        pltpu.make_async_copy(g, gz.at[zh], ls.at[2]),
        pltpu.make_async_copy(ogt.at[pl.ds(pl.multiple_of(zh * 56, 8), 56)], og_slot, ls.at[3]),
    ]
    used[0] = 4
    for q in own:
        q.start()

    barrier = pltpu.get_barrier_semaphore()
    for partner in plane + column + [peer(c, "k", 1)]:
        pl.semaphore_signal(barrier, inc=1, device_id=partner, device_id_type=MESH)

    @pl.when(jnp.logical_not(own_yz))
    def _():
        pl.semaphore_signal(barrier, inc=1, device_id=swap_yz, device_id_type=MESH)
        pl.semaphore_signal(barrier, inc=1, device_id=swap_yz_far, device_id_type=MESH)

    pl.semaphore_wait(barrier, 33 - jnp.where(own_yz, 2, 0))

    def gather_first(bufA, bufB, srcA=None, srcB=None):
        srcA = bufA.at[y, x] if srcA is None else srcA
        srcB = bufB.at[x, y] if srcB is None else srcB
        return to_peers("x", srcA, bufA.at[y, x]), to_peers("y", srcB, bufB.at[x, y])

    def gather_second(bufA, bufB, first):
        arrived(first[0])
        second = to_peers("y", bufA.at[y], bufA.at[y])
        arrived(first[1])
        return second + to_peers("x", bufB.at[x], bufB.at[x])

    class Pipeline:
        def __init__(self, buf, src, one, two):
            self.buf, self.src, self.one, self.two, self.sends = buf, src, one, two, {}

        def slot(self, d2, d1, rows=None):
            ref = self.buf.at[at_distance(c, self.two, d2), at_distance(c, self.one, d1)]
            return ref if rows is None else ref.at[pl.ds(*rows)]

        def go(self, key, src, dst, axis, d):
            self.sends[key] = start([remote(src, dst, peer(c, axis, d))])

        def spread(self, e):
            src = self.src if e == 0 else self.slot(0, e)
            for d in (1, 3):
                self.go(("spread", e, d), src, self.slot(0, e), self.two, d)

        def begin(self):
            for d in (1, 3):
                self.go(("own", d), self.src, self.slot(0, 0), self.one, d)
            self.spread(0)

        def relay(self):
            arrived(self.sends["own", 1] + self.sends["own", 3])
            for d, rows in ((1, (0, 56)), (3, (56, 56))):
                ref = self.slot(0, 4 - d, rows)
                self.go(("relay", d), ref, ref, self.one, d)
            self.spread(3)
            self.spread(1)

        def opposite(self):
            arrived(self.sends["relay", 1] + self.sends["relay", 3])
            self.spread(2)

        def forward(self, e):
            arrived(self.sends["spread", e, 1] + self.sends["spread", e, 3])
            for d, rows in ((1, (0, 56)), (3, (56, 56))):
                if e in (0, 2) or e == 4 - d:
                    ref = self.slot(4 - d, e, rows if e in (0, 2) else None)
                    self.go(("forward", e, d), ref, ref, self.two, d)

        def end(self):
            for key, q in self.sends.items():
                if key[0] == "forward":
                    arrived(q)

    class Ring:
        def __init__(self, buf):
            self.buf, self.step, self.last = buf, 0, None

        def advance(self, steps=1):
            for _ in range(steps):
                if self.last is not None:
                    arrived(self.last)
                s = self.step
                self.step += 1
                self.last = []
                for d in (1, -1):
                    if s < (8 if d == 1 else 7):
                        block = lax.rem(z - d * s + 16, 16)
                        ref = self.buf.at[block % 4, block // 4, k]
                        self.last += start([remote(ref, ref, along_z(d + 16))])

        def end(self):
            self.advance(8 - self.step)
            arrived(self.last)
            return start([remote(self.buf.at[:, :, k], self.buf.at[:, :, k], peer(c, "k", 1))])

    g1 = to_peers("zh", g, gz.at[zh])
    qb = start([Maybe(own_yz, bt, ball.at[y, zh, k], swap_yz)])
    oa = Pipeline(oA, o.at[pl.ds(0, 112)], "x", "y")
    ob = Pipeline(oB, o.at[pl.ds(112, 112)], "y", "x")
    oa.begin()
    ob.begin()
    a_slot = aAB.at[k, zl + k * (x - zl), x + k * (zl - x)]
    tokens_near = at.at[:, pl.ds(pl.multiple_of(k * 128, 128), 128)]
    tokens_far = at.at[:, pl.ds(pl.multiple_of((1 - k) * 128, 128), 128)]
    qa = start([Maybe(own_yz, tokens_near, a_slot, swap_yz), remote(tokens_far, a_slot, swap_yz_far)])
    for p in (oa, ob):
        p.relay()
    bring = Ring(ball)
    arrived(qb)
    bring.advance(1)
    for p in (oa, ob):
        p.forward(0)
    for q in own:
        q.wait()
    bring.advance(1)
    for p in (oa, ob):
        p.opposite()
    arrived(g1)
    g2 = start([remote(gz.at[at_distance(c, "x", d)], gall.at[x], peer(c, "x", d)) for d in ORDER])
    gall[x] = gz[x]
    qs = start([Maybe(own_yz, spt, spsw.at[k], swap_yz)])
    qog = start([
        remote(ogt.at[pl.ds(pl.multiple_of(at_distance(c, "zh", d) * 56, 8), 56)], og_slot, peer(c, "zh", d))
        for d in ORDER
    ])
    bring.advance(1)
    for p in (oa, ob):
        p.forward(3)
        p.forward(1)
    bring.advance(2)
    for p in (oa, ob):
        p.forward(2)
    arrived(qa)
    a1 = gather_first(aAB.at[0], aAB.at[1])
    bring.advance(1)

    arrived(g2)
    gcat = both(gall[...].reshape(896, 128), 1)
    for p in (oa, ob):
        p.end()

    def t_step(i, _):
        for j in range(4):
            for half, block in ((0, oA[i, j]), (1, oB[j, i])):
                hi, lo = split(block)
                ohi[i, j, half * 112 : half * 112 + 112] = hi
                olo[i, j, half * 112 : half * 112 + 112] = lo
        part = dot3(ohi[i].reshape(896, 448), olo[i].reshape(896, 448), gcat, ((0,), (0,)))
        tp[0, i] = part[:224]
        tp[1, i] = part[224:]
        return 0

    lax.fori_loop(0, 4, t_step, 0)
    t1 = start([remote(tp.at[1 - k], tk, peer(c, "k", 1))])
    a2 = gather_second(aAB.at[0], aAB.at[1], a1)
    arrived(t1)
    ts[...] = tp[k] + tk[...]
    t2 = scatter("zl", ts, tz)
    b4 = bring.end()
    arrived(b4)
    blocks = [(i, j) for i in range(4) for j in range(4)]
    btv = jnp.concatenate([ball[i, j].reshape(128, 128) for i, j in blocks], axis=1)
    bcat[...] = both(btv, 0)
    arrived(t2)
    tv = summed(ts[zl], tz)
    tA[y, x] = tv[:112]
    tB[x, y] = tv[112:]
    t3 = gather_first(tA, tB)
    t4 = gather_second(tA, tB, t3)

    arrived(a2)
    arows = jnp.concatenate([aAB[0, i, j] if h == 0 else aAB[1, j, i] for i, j in blocks for h in range(2)], axis=0)
    wall[zl, zh, k] = dot3(bcat[:128], bcat[128:], both(arows, 1))
    wring = Ring(wall)
    wring.advance(1)
    arrived(qs)
    arrived(start([remote(spsw.at[k], spsw.at[k], peer(c, "k", 1))]))
    sp_rows = jnp.concatenate([spsw[0], spsw[1]], axis=0).T + damping
    damped[0] = sp_rows[:224]
    damped[1] = sp_rows[224:]
    wring.advance(1)
    arrived(qog)
    og1 = gather_first(ogAB.at[0], ogAB.at[1])
    arrived(t4)

    trows = jnp.concatenate(
        [
            jnp.concatenate([tA[i, j] for i, j in blocks], axis=1),
            jnp.concatenate([tB[j, i] for i, j in blocks], axis=1),
        ],
        axis=0,
    )
    thi, tlo = split(trows)
    wide = mm(thi, bcat[...], ((1,), (1,)))
    rotated = wide[:, :128] + wide[:, 128:] + mm(tlo, bcat[:128], ((1,), (1,)))
    sall[zl, k] = rotated / damped[k]
    s1 = to_peers("zl", sall.at[zl, k], sall.at[zl, k])
    s2 = start([remote(sall.at[zl, k], sall.at[zl, k], peer(c, "k", 1))])
    for q, d in zip(s1, ORDER):
        arrived([q])
        origin = lax.rem(zl - d + 4, 4)
        s2 += start([remote(sall.at[origin, k], sall.at[origin, k], peer(c, "k", 1))])
    wring.advance(1)
    og2 = gather_second(ogAB.at[0], ogAB.at[1], og1)
    wring.advance(1)
    arrived(s2)

    scat[...] = both(sall[...].reshape(1792, 128), 1).reshape(4, 448, 256)

    def b_step(j, _):
        total = dot3(ohi[0, j], olo[0, j], scat[0])
        for i in range(1, 4):
            total = total + dot3(ohi[i, j], olo[i, j], scat[i])
        for q in range(4):
            bp[q, j] = total[q * 56 : q * 56 + 56]
        return 0

    lax.fori_loop(0, 4, b_step, 0)
    k1 = scatter("zh", bp, bz)
    w3 = wring.end()
    arrived(w3)

    def w_step(n, _):
        i, j = n // 4, n % 4
        hi, lo = split(jnp.concatenate([wall[i, j, 0], wall[i, j, 1]], axis=1))
        wcat[n, :128] = hi
        wcat[n, 128:256] = lo
        wcat[n, 256:] = hi
        return 0

    lax.fori_loop(0, 16, w_step, 0)
    arrived(og2)
    arrived(k1)
    khi, klo = split(summed(bp[zh], bz).reshape(224, 128))
    kcat = jnp.concatenate([khi, khi, klo], axis=1)

    def f_step(n, _):
        i, j = n // 4, n % 4
        m = mm(kcat, wcat[n])
        half = j // 2
        v = jnp.zeros((56, 256), F32)
        for n_x in range(4):
            v = v + m[n_x * 56 : n_x * 56 + 56] * ogAB[half, i + half * (n_x - i), n_x + half * (i - n_x), j % 2]
        f0[i, j] = jnp.sum(v.reshape(7, 8, 256), axis=0)
        return 0

    lax.fori_loop(0, 16, f_step, 0)
    row = lax.broadcasted_iota(jnp.int32, (8, 256), 0)
    for i in range(4):
        line = jnp.zeros((8, 256), F32)
        for j in range(4):
            line = jnp.where(row == j, jnp.sum(f0[i, j], axis=0, keepdims=True), line)
        f1[i] = line
    got = []
    for n, partner in enumerate(plane):
        i, j = (n + 1) // 4, (n + 1) % 4
        got += start([remote(f1.at[at_distance(c, "y", j)], f2.at[x, y], partner)])
    f2[x, y] = f1[y]
    arrived(got)
    total = jnp.sum(f2[...].reshape(16, 8, 256), axis=0)
    for j in range(4):
        f3[j] = jnp.broadcast_to(total[j : j + 1], (8, 256))
    got = []
    for n, partner in enumerate(column):
        i, j = (n + 1) // 4, (n + 1) % 4
        got += start([remote(f3.at[at_distance(c, "zh", j)], f4.at[k, zl, zh], partner)])
    f4[k, zl, zh] = f3[zh]
    arrived(got)
    f5[k] = jnp.sum(f4[k].reshape(16, 8, 256), axis=0)
    arrived(start([remote(f5.at[k], f5.at[k], peer(c, "k", 1))]))
    out[...] = (f5[0] + f5[1])[:1]
    for q in sent:
        q.wait_send()


def body(query_grad, basis_in, basis_out, spectrum, activations, out_grads):
    def vmem(*shape, dtype=F32):
        return pltpu.VMEM(shape, dtype)

    out = pl.pallas_call(
        kernel,
        out_shape=jax.ShapeDtypeStruct((1, 256), F32),
        in_specs=[pl.BlockSpec(memory_space=pl.ANY)] * 6,
        out_specs=pl.BlockSpec(memory_space=pltpu.VMEM),
        scratch_shapes=[
            vmem(4, 4, 112, 448),
            vmem(4, 4, 112, 448),
            vmem(4, 4, 224, 448, dtype=BF16),
            vmem(4, 4, 224, 448, dtype=BF16),
            vmem(4, 224, 128),
            vmem(4, 224, 128),
            vmem(2, 64, 448),
            vmem(2, 224, 128),
            vmem(4, 4, 2, 64, 128),
            vmem(256, 2048, dtype=BF16),
            vmem(2, 4, 4, 64, 128),
            vmem(4, 4, 2, 128, 128),
            vmem(16, 384, 256, dtype=BF16),
            vmem(2, 4, 4, 2, 56, 256),
            vmem(2, 4, 224, 128),
            vmem(4, 224, 128),
            vmem(4, 224, 128),
            vmem(4, 224, 128),
            vmem(4, 4, 112, 128),
            vmem(4, 4, 112, 128),
            vmem(4, 2, 224, 128),
            vmem(4, 448, 256, dtype=BF16),
            vmem(4, 4, 56, 128),
            vmem(4, 4, 56, 128),
            vmem(4, 4, 8, 256),
            vmem(4, 8, 256),
            vmem(4, 4, 8, 256),
            vmem(4, 8, 256),
            vmem(2, 4, 4, 8, 256),
            vmem(2, 8, 256),
            pltpu.SemaphoreType.DMA((N_SEMS,)),
            pltpu.SemaphoreType.DMA((N_SEMS,)),
            pltpu.SemaphoreType.DMA((N_SEMS,)),
        ],
        compiler_params=pltpu.CompilerParams(
            collective_id=0, has_side_effects=True, vmem_limit_bytes=56 * 1024 * 1024
        ),
    )(query_grad, basis_in.T, basis_out, spectrum.T, activations.T, out_grads.T)
    return out.reshape(256)


def solution(mesh):
    in_specs = (
        P("eig", "tok"),
        P("tok", "eig"),
        P("eig", "tok"),
        P("tok", "eig"),
        P("tok", "eig"),
        P("tok", "eig"),
    )
    out_specs = P("tok")
    return jax.shard_map(body, mesh=mesh, in_specs=in_specs, out_specs=out_specs, check_vma=False)
```

```python
import jax
import jax.numpy as jnp
from jax import lax
from jax.experimental import pallas as pl
from jax.experimental.pallas import tpu as pltpu
from jax.sharding import PartitionSpec as P

damping = 0.1
MESH = pl.DeviceIdType.MESH
F32, BF16 = jnp.float32, jnp.bfloat16
SIZE = dict(zl=4, x=4, k=2, y=4, zh=4)
N_SEMS = 256
ORDER = (1, 3, 2)


def coords():
    e, t = lax.axis_index("eig"), lax.axis_index("tok")
    return dict(zl=e // 8, x=(e // 2) % 4, k=e % 2, y=t // 4, zh=t % 4)


def place(c, **other):
    d = dict(c, **other)
    return (d["zl"] * 8 + d["x"] * 2 + d["k"], d["y"] * 4 + d["zh"])


def peer(c, axis, d):
    return place(c, **{axis: lax.rem(c[axis] + d, SIZE[axis])})


def at_distance(c, axis, d):
    return lax.rem(c[axis] + d, SIZE[axis])


def split(v):
    hi = v.astype(BF16)
    return hi, (v - hi.astype(F32)).astype(BF16)


def mm(left, right, dims=((1,), (0,))):
    return lax.dot_general(left, right, (dims, ((), ())), preferred_element_type=F32)


def dot3(lh, ll, cat, dims=((1,), (0,))):
    n = cat.shape[1] // 2
    wide = mm(lh, cat, dims)
    return wide[:, :n] + wide[:, n:] + mm(ll, cat[:, :n], dims)


def both(v, axis):
    return jnp.concatenate(split(v), axis=axis)


def kernel(
    g, bt, o, spt, at, ogt, out,
    oA, oB, ohi, olo, gz, gall, spsw, damped, ball, bcat, aAB, wall, wcat, ogAB,
    tp, tk, ts, tz, tA, tB, sall, scat, bp, bz, f0, f1, f2, f3, f4, f5,
    ss, rs, ls,
):
    c = coords()
    x, y, zl, zh, k = c["x"], c["y"], c["zl"], c["zh"], c["k"]
    used = [0]
    sent = []

    def remote(src, dst, device):
        i = used[0]
        used[0] += 1
        return pltpu.make_async_remote_copy(
            src_ref=src, dst_ref=dst, send_sem=ss.at[i], recv_sem=rs.at[i], device_id=device, device_id_type=MESH
        )

    def start(copies):
        for q in copies:
            q.start()
            sent.append(q)
        return copies

    def arrived(copies):
        for q in copies:
            q.wait_recv()

    class Maybe:
        def __init__(self, own, src, dst, device):
            self.own, self.far = own, remote(src, dst, device)
            self.near = pltpu.make_async_copy(src, dst, ls.at[used[0]])

        def start(self):
            pl.when(jnp.logical_not(self.own))(self.far.start)
            pl.when(self.own)(self.near.start)

        def wait_recv(self):
            pl.when(jnp.logical_not(self.own))(self.far.wait_recv)
            pl.when(self.own)(self.near.wait)

        def wait_send(self):
            pl.when(jnp.logical_not(self.own))(self.far.wait_send)

    def to_peers(axis, src, dst):
        return start([remote(src, dst, peer(c, axis, d)) for d in ORDER])

    def scatter(axis, src, dst):
        return start([remote(src.at[at_distance(c, axis, d)], dst.at[d], peer(c, axis, d)) for d in ORDER])

    def summed(own, got):
        return own + got[1] + got[2] + got[3]

    swap_yz = place(c, y=zl, zl=y)
    swap_yz_far = place(c, y=zl, zl=y, k=1 - k)
    own_yz = y == zl
    plane = [
        place(c, x=at_distance(c, "x", i), y=at_distance(c, "y", j)) for i in range(4) for j in range(4) if i or j
    ]
    column = [
        place(c, zl=at_distance(c, "zl", i), zh=at_distance(c, "zh", j)) for i in range(4) for j in range(4) if i or j
    ]
    z = zh * 4 + zl

    def along_z(d):
        other = lax.rem(z + d, 16)
        return place(c, zl=other % 4, zh=other // 4)

    og_half = zh // 2
    og_slot = ogAB.at[og_half, y + og_half * (x - y), x + og_half * (y - x), zh % 2]

    own = [
        pltpu.make_async_copy(o.at[pl.ds(0, 112)], oA.at[y, x], ls.at[0]),
        pltpu.make_async_copy(o.at[pl.ds(112, 112)], oB.at[x, y], ls.at[1]),
        pltpu.make_async_copy(g, gz.at[zh], ls.at[2]),
        pltpu.make_async_copy(ogt.at[pl.ds(pl.multiple_of(zh * 56, 8), 56)], og_slot, ls.at[3]),
    ]
    used[0] = 4
    for q in own:
        q.start()

    barrier = pltpu.get_barrier_semaphore()
    for partner in plane + column + [peer(c, "k", 1)]:
        pl.semaphore_signal(barrier, inc=1, device_id=partner, device_id_type=MESH)

    @pl.when(jnp.logical_not(own_yz))
    def _():
        pl.semaphore_signal(barrier, inc=1, device_id=swap_yz, device_id_type=MESH)
        pl.semaphore_signal(barrier, inc=1, device_id=swap_yz_far, device_id_type=MESH)

    pl.semaphore_wait(barrier, 33 - jnp.where(own_yz, 2, 0))

    def gather_first(bufA, bufB, srcA=None, srcB=None):
        srcA = bufA.at[y, x] if srcA is None else srcA
        srcB = bufB.at[x, y] if srcB is None else srcB
        return to_peers("x", srcA, bufA.at[y, x]), to_peers("y", srcB, bufB.at[x, y])

    def gather_second(bufA, bufB, first):
        arrived(first[0])
        second = to_peers("y", bufA.at[y], bufA.at[y])
        arrived(first[1])
        return second + to_peers("x", bufB.at[x], bufB.at[x])

    class Pipeline:
        def __init__(self, buf, src, one, two):
            self.buf, self.src, self.one, self.two, self.sends = buf, src, one, two, {}

        def slot(self, d2, d1, rows=None):
            ref = self.buf.at[at_distance(c, self.two, d2), at_distance(c, self.one, d1)]
            return ref if rows is None else ref.at[pl.ds(*rows)]

        def go(self, key, src, dst, axis, d):
            self.sends[key] = start([remote(src, dst, peer(c, axis, d))])

        def spread(self, e):
            src = self.src if e == 0 else self.slot(0, e)
            for d in (1, 3):
                self.go(("spread", e, d), src, self.slot(0, e), self.two, d)

        def begin(self):
            for d in (1, 3):
                self.go(("own", d), self.src, self.slot(0, 0), self.one, d)
            self.spread(0)

        def relay(self):
            arrived(self.sends["own", 1] + self.sends["own", 3])
            for d, rows in ((1, (0, 56)), (3, (56, 56))):
                ref = self.slot(0, 4 - d, rows)
                self.go(("relay", d), ref, ref, self.one, d)
            self.spread(3)
            self.spread(1)

        def opposite(self):
            arrived(self.sends["relay", 1] + self.sends["relay", 3])
            self.spread(2)

        def forward(self, e):
            arrived(self.sends["spread", e, 1] + self.sends["spread", e, 3])
            for d, rows in ((1, (0, 56)), (3, (56, 56))):
                if e in (0, 2) or e == 4 - d:
                    ref = self.slot(4 - d, e, rows if e in (0, 2) else None)
                    self.go(("forward", e, d), ref, ref, self.two, d)

        def end(self):
            for key, q in self.sends.items():
                if key[0] == "forward":
                    arrived(q)

    class Ring:
        def __init__(self, buf):
            self.buf, self.step, self.last = buf, 0, None

        def advance(self, steps=1):
            for _ in range(steps):
                if self.last is not None:
                    arrived(self.last)
                s = self.step
                self.step += 1
                self.last = []
                for d in (1, -1):
                    if s < (8 if d == 1 else 7):
                        block = lax.rem(z - d * s + 16, 16)
                        ref = self.buf.at[block % 4, block // 4, k]
                        self.last += start([remote(ref, ref, along_z(d + 16))])

        def end(self):
            self.advance(8 - self.step)
            arrived(self.last)
            return start([remote(self.buf.at[:, :, k], self.buf.at[:, :, k], peer(c, "k", 1))])

    g1 = to_peers("zh", g, gz.at[zh])
    qb = start([Maybe(own_yz, bt, ball.at[y, zh, k], swap_yz)])
    oa = Pipeline(oA, o.at[pl.ds(0, 112)], "x", "y")
    ob = Pipeline(oB, o.at[pl.ds(112, 112)], "y", "x")
    oa.begin()
    ob.begin()
    a_slot = aAB.at[k, zl + k * (x - zl), x + k * (zl - x)]
    tokens_near = at.at[:, pl.ds(pl.multiple_of(k * 128, 128), 128)]
    tokens_far = at.at[:, pl.ds(pl.multiple_of((1 - k) * 128, 128), 128)]
    qa = start([Maybe(own_yz, tokens_near, a_slot, swap_yz), remote(tokens_far, a_slot, swap_yz_far)])
    for p in (oa, ob):
        p.relay()
    for p in (oa, ob):
        p.forward(0)
    for q in own:
        q.wait()
    for p in (oa, ob):
        p.opposite()
    arrived(g1)
    g2 = start([remote(gz.at[at_distance(c, "x", d)], gall.at[x], peer(c, "x", d)) for d in ORDER])
    gall[x] = gz[x]
    bring = Ring(ball)
    arrived(qb)
    bring.advance(1)
    for p in (oa, ob):
        p.forward(3)
        p.forward(1)
    bring.advance(2)
    arrived(qa)
    a1 = gather_first(aAB.at[0], aAB.at[1])
    for p in (oa, ob):
        p.forward(2)
    bring.advance(1)
    qs = start([Maybe(own_yz, spt, spsw.at[k], swap_yz)])
    qog = start([
        remote(ogt.at[pl.ds(pl.multiple_of(at_distance(c, "zh", d) * 56, 8), 56)], og_slot, peer(c, "zh", d))
        for d in ORDER
    ])
    a2 = gather_second(aAB.at[0], aAB.at[1], a1)

    def convert(half, i, j):
        hi, lo = split(oA[i, j] if half == 0 else oB[j, i])
        ohi[i, j, half * 112 : half * 112 + 112] = hi
        olo[i, j, half * 112 : half * 112 + 112] = lo

    def early(n, _):
        for d in (0, 1, 3):
            convert(0, at_distance(c, "y", d), n)
            convert(1, n, at_distance(c, "x", d))
        return 0

    def late(n, _):
        convert(0, at_distance(c, "y", 2), n)
        convert(1, n, at_distance(c, "x", 2))
        return 0

    lax.fori_loop(0, 4, early, 0)
    bring.advance(1)

    arrived(g2)
    gcat = both(gall[...].reshape(896, 128), 1)
    for p in (oa, ob):
        p.end()
    lax.fori_loop(0, 4, late, 0)

    def t_step(i, _):
        part = dot3(ohi[i].reshape(896, 448), olo[i].reshape(896, 448), gcat, ((0,), (0,)))
        tp[0, i] = part[:224]
        tp[1, i] = part[224:]
        return 0

    lax.fori_loop(0, 4, t_step, 0)
    t1 = start([remote(tp.at[1 - k], tk, peer(c, "k", 1))])
    bring.advance(1)
    arrived(t1)
    ts[...] = tp[k] + tk[...]
    t2 = scatter("zl", ts, tz)
    arrived(bring.end())
    blocks = [(i, j) for i in range(4) for j in range(4)]
    btv = jnp.concatenate([ball[i, j].reshape(128, 128) for i, j in blocks], axis=1)
    bcat[...] = both(btv, 0)

    arrived(a2)
    arows = jnp.concatenate([aAB[0, i, j] if h == 0 else aAB[1, j, i] for i, j in blocks for h in range(2)], axis=0)
    wall[zl, zh, k] = dot3(bcat[:128], bcat[128:], both(arows, 1))
    wring = Ring(wall)
    wring.advance(1)
    arrived(t2)
    tv = summed(ts[zl], tz)
    tA[y, x] = tv[:112]
    tB[x, y] = tv[112:]
    t3 = gather_first(tA, tB)
    wring.advance(1)
    t4 = gather_second(tA, tB, t3)
    wring.advance(2)
    arrived(qs)
    arrived(start([remote(spsw.at[k], spsw.at[k], peer(c, "k", 1))]))
    sp_rows = jnp.concatenate([spsw[0], spsw[1]], axis=0).T + damping
    damped[0] = sp_rows[:224]
    damped[1] = sp_rows[224:]
    wring.advance(1)
    arrived(qog)
    og1 = gather_first(ogAB.at[0], ogAB.at[1])
    arrived(t4)

    trows = jnp.concatenate(
        [
            jnp.concatenate([tA[i, j] for i, j in blocks], axis=1),
            jnp.concatenate([tB[j, i] for i, j in blocks], axis=1),
        ],
        axis=0,
    )
    thi, tlo = split(trows)
    wide = mm(thi, bcat[...], ((1,), (1,)))
    rotated = wide[:, :128] + wide[:, 128:] + mm(tlo, bcat[:128], ((1,), (1,)))
    sall[zl, k] = rotated / damped[k]
    s1 = to_peers("zl", sall.at[zl, k], sall.at[zl, k])
    s2 = start([remote(sall.at[zl, k], sall.at[zl, k], peer(c, "k", 1))])
    wring.advance(1)
    og2 = gather_second(ogAB.at[0], ogAB.at[1], og1)
    for q, d in zip(s1, ORDER):
        arrived([q])
        origin = lax.rem(zl - d + 4, 4)
        s2 += start([remote(sall.at[origin, k], sall.at[origin, k], peer(c, "k", 1))])
    arrived(s2)

    scat[...] = both(sall[...].reshape(1792, 128), 1).reshape(4, 448, 256)

    def b_step(j, _):
        total = dot3(ohi[0, j], olo[0, j], scat[0])
        for i in range(1, 4):
            total = total + dot3(ohi[i, j], olo[i, j], scat[i])
        for q in range(4):
            bp[q, j] = total[q * 56 : q * 56 + 56]
        return 0

    lax.fori_loop(0, 4, b_step, 0)
    k1 = scatter("zh", bp, bz)
    w3 = wring.end()
    arrived(w3)

    def w_step(n, _):
        i, j = n // 4, n % 4
        hi, lo = split(jnp.concatenate([wall[i, j, 0], wall[i, j, 1]], axis=1))
        wcat[n, :128] = hi
        wcat[n, 128:256] = lo
        wcat[n, 256:] = hi
        return 0

    lax.fori_loop(0, 16, w_step, 0)
    arrived(og2)
    arrived(k1)
    khi, klo = split(summed(bp[zh], bz).reshape(224, 128))
    kcat = jnp.concatenate([khi, khi, klo], axis=1)

    def f_step(n, _):
        i, j = n // 4, n % 4
        m = mm(kcat, wcat[n])
        half = j // 2
        v = jnp.zeros((56, 256), F32)
        for n_x in range(4):
            v = v + m[n_x * 56 : n_x * 56 + 56] * ogAB[half, i + half * (n_x - i), n_x + half * (i - n_x), j % 2]
        f0[i, j] = jnp.sum(v.reshape(7, 8, 256), axis=0)
        return 0

    lax.fori_loop(0, 16, f_step, 0)
    row = lax.broadcasted_iota(jnp.int32, (8, 256), 0)
    for i in range(4):
        line = jnp.zeros((8, 256), F32)
        for j in range(4):
            line = jnp.where(row == j, jnp.sum(f0[i, j], axis=0, keepdims=True), line)
        f1[i] = line
    got = []
    for n, partner in enumerate(plane):
        i, j = (n + 1) // 4, (n + 1) % 4
        got += start([remote(f1.at[at_distance(c, "y", j)], f2.at[x, y], partner)])
    f2[x, y] = f1[y]
    arrived(got)
    total = jnp.sum(f2[...].reshape(16, 8, 256), axis=0)
    for j in range(4):
        f3[j] = total[j : j + 1]
    got = []
    for n, partner in enumerate(column):
        i, j = (n + 1) // 4, (n + 1) % 4
        got += start([remote(f3.at[at_distance(c, "zh", j)], f4.at[k, zl, zh], partner)])
    f4[k, zl, zh] = f3[zh]
    arrived(got)
    f5[k] = jnp.sum(f4[k].reshape(16, 1, 256), axis=0)
    arrived(start([remote(f5.at[k], f5.at[k], peer(c, "k", 1))]))
    out[...] = f5[0] + f5[1]
    for q in sent:
        q.wait_send()


def body(query_grad, basis_in, basis_out, spectrum, activations, out_grads):
    def vmem(*shape, dtype=F32):
        return pltpu.VMEM(shape, dtype)

    out = pl.pallas_call(
        kernel,
        out_shape=jax.ShapeDtypeStruct((1, 256), F32),
        in_specs=[pl.BlockSpec(memory_space=pl.ANY)] * 6,
        out_specs=pl.BlockSpec(memory_space=pltpu.VMEM),
        scratch_shapes=[
            vmem(4, 4, 112, 448),
            vmem(4, 4, 112, 448),
            vmem(4, 4, 224, 448, dtype=BF16),
            vmem(4, 4, 224, 448, dtype=BF16),
            vmem(4, 224, 128),
            vmem(4, 224, 128),
            vmem(2, 64, 448),
            vmem(2, 224, 128),
            vmem(4, 4, 2, 64, 128),
            vmem(256, 2048, dtype=BF16),
            vmem(2, 4, 4, 64, 128),
            vmem(4, 4, 2, 128, 128),
            vmem(16, 384, 256, dtype=BF16),
            vmem(2, 4, 4, 2, 56, 256),
            vmem(2, 4, 224, 128),
            vmem(4, 224, 128),
            vmem(4, 224, 128),
            vmem(4, 224, 128),
            vmem(4, 4, 112, 128),
            vmem(4, 4, 112, 128),
            vmem(4, 2, 224, 128),
            vmem(4, 448, 256, dtype=BF16),
            vmem(4, 4, 56, 128),
            vmem(4, 4, 56, 128),
            vmem(4, 4, 8, 256),
            vmem(4, 8, 256),
            vmem(4, 4, 8, 256),
            vmem(4, 1, 256),
            vmem(2, 4, 4, 1, 256),
            vmem(2, 1, 256),
            pltpu.SemaphoreType.DMA((N_SEMS,)),
            pltpu.SemaphoreType.DMA((N_SEMS,)),
            pltpu.SemaphoreType.DMA((N_SEMS,)),
        ],
        compiler_params=pltpu.CompilerParams(
            collective_id=0, has_side_effects=True, vmem_limit_bytes=56 * 1024 * 1024
        ),
    )(query_grad, basis_in.T, basis_out, spectrum.T, activations.T, out_grads.T)
    return out.reshape(256)


def solution(mesh):
    in_specs = (
        P("eig", "tok"),
        P("tok", "eig"),
        P("eig", "tok"),
        P("tok", "eig"),
        P("tok", "eig"),
        P("tok", "eig"),
    )
    out_specs = P("tok")
    return jax.shard_map(body, mesh=mesh, in_specs=in_specs, out_specs=out_specs, check_vma=False)
```

```python
import jax
import jax.numpy as jnp
from jax import lax
from jax.experimental import pallas as pl
from jax.experimental.pallas import tpu as pltpu
from jax.sharding import PartitionSpec as P

damping = 0.1
MESH = pl.DeviceIdType.MESH
F32, BF16 = jnp.float32, jnp.bfloat16
SIZE = dict(zl=4, x=4, k=2, y=4, zh=4)
N_SEMS = 256
ORDER = (1, 3, 2)


def coords():
    e, t = lax.axis_index("eig"), lax.axis_index("tok")
    return dict(zl=e // 8, x=(e // 2) % 4, k=e % 2, y=t // 4, zh=t % 4)


def place(c, **other):
    d = dict(c, **other)
    return (d["zl"] * 8 + d["x"] * 2 + d["k"], d["y"] * 4 + d["zh"])


def peer(c, axis, d):
    return place(c, **{axis: lax.rem(c[axis] + d, SIZE[axis])})


def at_distance(c, axis, d):
    return lax.rem(c[axis] + d, SIZE[axis])


def split(v):
    hi = v.astype(BF16)
    return hi, (v - hi.astype(F32)).astype(BF16)


def mm(left, right, dims=((1,), (0,))):
    return lax.dot_general(left, right, (dims, ((), ())), preferred_element_type=F32)


def dot3(lh, ll, cat, dims=((1,), (0,))):
    n = cat.shape[1] // 2
    wide = mm(lh, cat, dims)
    return wide[:, :n] + wide[:, n:] + mm(ll, cat[:, :n], dims)


def both(v, axis):
    return jnp.concatenate(split(v), axis=axis)


def kernel(
    g, bt, o, spt, at, ogt, out,
    oA, oB, ohi, olo, gz, gall, spsw, damped, ball, bcat, aAB, wall, wcat, ogAB,
    tp, tk, ts, tz, tA, tB, sall, scat, bp, bz, f0, f1, f2, f3, f4, f5,
    ss, rs, ls,
):
    c = coords()
    x, y, zl, zh, k = c["x"], c["y"], c["zl"], c["zh"], c["k"]
    used = [0]
    sent = []

    def remote(src, dst, device):
        i = used[0]
        used[0] += 1
        return pltpu.make_async_remote_copy(
            src_ref=src, dst_ref=dst, send_sem=ss.at[i], recv_sem=rs.at[i], device_id=device, device_id_type=MESH
        )

    def start(copies):
        for q in copies:
            q.start()
            sent.append(q)
        return copies

    def arrived(copies):
        for q in copies:
            q.wait_recv()

    class Maybe:
        def __init__(self, own, src, dst, device):
            self.own, self.far = own, remote(src, dst, device)
            self.near = pltpu.make_async_copy(src, dst, ls.at[used[0]])

        def start(self):
            pl.when(jnp.logical_not(self.own))(self.far.start)
            pl.when(self.own)(self.near.start)

        def wait_recv(self):
            pl.when(jnp.logical_not(self.own))(self.far.wait_recv)
            pl.when(self.own)(self.near.wait)

        def wait_send(self):
            pl.when(jnp.logical_not(self.own))(self.far.wait_send)

    def to_peers(axis, src, dst):
        return start([remote(src, dst, peer(c, axis, d)) for d in ORDER])

    def scatter(axis, src, dst):
        return start([remote(src.at[at_distance(c, axis, d)], dst.at[d], peer(c, axis, d)) for d in ORDER])

    def summed(own, got):
        return own + got[1] + got[2] + got[3]

    swap_yz = place(c, y=zl, zl=y)
    swap_yz_far = place(c, y=zl, zl=y, k=1 - k)
    own_yz = y == zl
    plane = [
        place(c, x=at_distance(c, "x", i), y=at_distance(c, "y", j)) for i in range(4) for j in range(4) if i or j
    ]
    column = [
        place(c, zl=at_distance(c, "zl", i), zh=at_distance(c, "zh", j)) for i in range(4) for j in range(4) if i or j
    ]
    z = zh * 4 + zl

    def along_z(d):
        other = lax.rem(z + d, 16)
        return place(c, zl=other % 4, zh=other // 4)

    og_half = zh // 2
    og_slot = ogAB.at[og_half, y + og_half * (x - y), x + og_half * (y - x), zh % 2]

    own = [
        pltpu.make_async_copy(o.at[pl.ds(0, 112)], oA.at[y, x], ls.at[0]),
        pltpu.make_async_copy(o.at[pl.ds(112, 112)], oB.at[x, y], ls.at[1]),
        pltpu.make_async_copy(g, gz.at[zh], ls.at[2]),
        pltpu.make_async_copy(ogt.at[pl.ds(pl.multiple_of(zh * 56, 8), 56)], og_slot, ls.at[3]),
    ]
    used[0] = 4
    for q in own:
        q.start()

    barrier = pltpu.get_barrier_semaphore()
    for partner in plane + column + [peer(c, "k", 1)]:
        pl.semaphore_signal(barrier, inc=1, device_id=partner, device_id_type=MESH)

    @pl.when(jnp.logical_not(own_yz))
    def _():
        pl.semaphore_signal(barrier, inc=1, device_id=swap_yz, device_id_type=MESH)
        pl.semaphore_signal(barrier, inc=1, device_id=swap_yz_far, device_id_type=MESH)

    pl.semaphore_wait(barrier, 33 - jnp.where(own_yz, 2, 0))

    def gather_first(bufA, bufB, srcA=None, srcB=None):
        srcA = bufA.at[y, x] if srcA is None else srcA
        srcB = bufB.at[x, y] if srcB is None else srcB
        return to_peers("x", srcA, bufA.at[y, x]), to_peers("y", srcB, bufB.at[x, y])

    def gather_second(bufA, bufB, first):
        arrived(first[0])
        second = to_peers("y", bufA.at[y], bufA.at[y])
        arrived(first[1])
        return second + to_peers("x", bufB.at[x], bufB.at[x])

    class Pipeline:
        def __init__(self, buf, src, one, two):
            self.buf, self.src, self.one, self.two, self.sends = buf, src, one, two, {}

        def slot(self, d2, d1, rows=None):
            ref = self.buf.at[at_distance(c, self.two, d2), at_distance(c, self.one, d1)]
            return ref if rows is None else ref.at[pl.ds(*rows)]

        def go(self, key, src, dst, axis, d):
            self.sends[key] = start([remote(src, dst, peer(c, axis, d))])

        def spread(self, e):
            src = self.src if e == 0 else self.slot(0, e)
            for d in (1, 3):
                self.go(("spread", e, d), src, self.slot(0, e), self.two, d)

        def begin(self):
            for d in (1, 3):
                self.go(("own", d), self.src, self.slot(0, 0), self.one, d)
            self.spread(0)

        def relay(self):
            arrived(self.sends["own", 1] + self.sends["own", 3])
            for d, rows in ((1, (0, 56)), (3, (56, 56))):
                ref = self.slot(0, 4 - d, rows)
                self.go(("relay", d), ref, ref, self.one, d)
            self.spread(3)
            self.spread(1)

        def opposite(self):
            arrived(self.sends["relay", 1] + self.sends["relay", 3])
            self.spread(2)

        def forward(self, e):
            arrived(self.sends["spread", e, 1] + self.sends["spread", e, 3])
            for d, rows in ((1, (0, 56)), (3, (56, 56))):
                if e in (0, 2) or e == 4 - d:
                    ref = self.slot(4 - d, e, rows if e in (0, 2) else None)
                    self.go(("forward", e, d), ref, ref, self.two, d)

        def end(self):
            for key, q in self.sends.items():
                if key[0] == "forward":
                    arrived(q)

    class Ring:
        def __init__(self, buf):
            self.buf, self.step, self.last = buf, 0, None

        def advance(self, steps=1):
            for _ in range(steps):
                if self.last is not None:
                    arrived(self.last)
                s = self.step
                self.step += 1
                self.last = []
                for d in (1, -1):
                    if s < (8 if d == 1 else 7):
                        block = lax.rem(z - d * s + 16, 16)
                        ref = self.buf.at[block % 4, block // 4, k]
                        self.last += start([remote(ref, ref, along_z(d + 16))])

        def end(self):
            self.advance(8 - self.step)
            arrived(self.last)
            return start([remote(self.buf.at[:, :, k], self.buf.at[:, :, k], peer(c, "k", 1))])

    g1 = to_peers("zh", g, gz.at[zh])
    qb = start([Maybe(own_yz, bt, ball.at[y, zh, k], swap_yz)])
    oa = Pipeline(oA, o.at[pl.ds(0, 112)], "x", "y")
    ob = Pipeline(oB, o.at[pl.ds(112, 112)], "y", "x")
    oa.begin()
    ob.begin()
    a_slot = aAB.at[k, zl + k * (x - zl), x + k * (zl - x)]
    tokens_near = at.at[:, pl.ds(pl.multiple_of(k * 128, 128), 128)]
    tokens_far = at.at[:, pl.ds(pl.multiple_of((1 - k) * 128, 128), 128)]
    qa = start([Maybe(own_yz, tokens_near, a_slot, swap_yz), remote(tokens_far, a_slot, swap_yz_far)])
    for p in (oa, ob):
        p.relay()
    for p in (oa, ob):
        p.forward(0)
    for q in own:
        q.wait()
    for p in (oa, ob):
        p.opposite()
    arrived(g1)
    g2 = start([remote(gz.at[at_distance(c, "x", d)], gall.at[x], peer(c, "x", d)) for d in ORDER])
    gall[x] = gz[x]
    bring = Ring(ball)
    arrived(qb)
    bring.advance(1)
    for p in (oa, ob):
        p.forward(3)
        p.forward(1)
    bring.advance(2)
    arrived(qa)
    a1 = gather_first(aAB.at[0], aAB.at[1])
    for p in (oa, ob):
        p.forward(2)
    bring.advance(1)
    qs = start([Maybe(own_yz, spt, spsw.at[k], swap_yz)])
    qog = start([
        remote(ogt.at[pl.ds(pl.multiple_of(at_distance(c, "zh", d) * 56, 8), 56)], og_slot, peer(c, "zh", d))
        for d in ORDER
    ])
    a2 = gather_second(aAB.at[0], aAB.at[1], a1)

    def convert(half, i, j):
        hi, lo = split(oA[i, j] if half == 0 else oB[j, i])
        ohi[i, j, half * 112 : half * 112 + 112] = hi
        olo[i, j, half * 112 : half * 112 + 112] = lo

    def early(n, _):
        for d in (0, 1, 3):
            convert(0, at_distance(c, "y", d), n)
            convert(1, n, at_distance(c, "x", d))
        return 0

    def late(n, _):
        convert(0, at_distance(c, "y", 2), n)
        convert(1, n, at_distance(c, "x", 2))
        return 0

    lax.fori_loop(0, 4, early, 0)
    bring.advance(1)

    arrived(g2)
    gcat = both(gall[...].reshape(896, 128), 1)
    for p in (oa, ob):
        p.end()
    lax.fori_loop(0, 4, late, 0)

    def t_step(i, _):
        part = dot3(ohi[i].reshape(896, 448), olo[i].reshape(896, 448), gcat, ((0,), (0,)))
        tp[0, i] = part[:224]
        tp[1, i] = part[224:]
        return 0

    lax.fori_loop(0, 4, t_step, 0)
    t1 = start([remote(tp.at[1 - k], tk, peer(c, "k", 1))])
    bring.advance(1)
    arrived(t1)
    ts[...] = tp[k] + tk[...]
    t2 = scatter("zl", ts, tz)
    arrived(bring.end())
    blocks = [(i, j) for i in range(4) for j in range(4)]
    btv = jnp.concatenate([ball[i, j].reshape(128, 128) for i, j in blocks], axis=1)
    bcat[...] = both(btv, 0)

    arrived(a2)
    arows = jnp.concatenate([aAB[0, i, j] if h == 0 else aAB[1, j, i] for i, j in blocks for h in range(2)], axis=0)
    wall[zl, zh, k] = dot3(bcat[:128], bcat[128:], both(arows, 1))
    wring = Ring(wall)
    wring.advance(1)
    arrived(t2)
    tv = summed(ts[zl], tz)
    tA[y, x] = tv[:112]
    tB[x, y] = tv[112:]
    t3 = gather_first(tA, tB)
    wring.advance(1)
    t4 = gather_second(tA, tB, t3)
    wring.advance(2)
    arrived(qs)
    arrived(start([remote(spsw.at[k], spsw.at[k], peer(c, "k", 1))]))
    sp_rows = jnp.concatenate([spsw[0], spsw[1]], axis=0).T + damping
    damped[0] = sp_rows[:224]
    damped[1] = sp_rows[224:]
    wring.advance(1)
    arrived(qog)
    og1 = gather_first(ogAB.at[0], ogAB.at[1])
    arrived(t4)

    trows = jnp.concatenate(
        [
            jnp.concatenate([tA[i, j] for i, j in blocks], axis=1),
            jnp.concatenate([tB[j, i] for i, j in blocks], axis=1),
        ],
        axis=0,
    )
    thi, tlo = split(trows)
    wide = mm(thi, bcat[...], ((1,), (1,)))
    rotated = wide[:, :128] + wide[:, 128:] + mm(tlo, bcat[:128], ((1,), (1,)))
    sall[zl, k] = rotated / damped[k]
    s1 = to_peers("zl", sall.at[zl, k], sall.at[zl, k])
    s2 = start([remote(sall.at[zl, k], sall.at[zl, k], peer(c, "k", 1))])
    og2 = gather_second(ogAB.at[0], ogAB.at[1], og1)
    wring.advance(2)
    for q, d in zip(s1, ORDER):
        arrived([q])
        origin = lax.rem(zl - d + 4, 4)
        s2 += start([remote(sall.at[origin, k], sall.at[origin, k], peer(c, "k", 1))])
    arrived(s2)

    scat[...] = both(sall[...].reshape(1792, 128), 1).reshape(4, 448, 256)

    def b_step(j, _):
        total = dot3(ohi[0, j], olo[0, j], scat[0])
        for i in range(1, 4):
            total = total + dot3(ohi[i, j], olo[i, j], scat[i])
        for q in range(4):
            bp[q, j] = total[q * 56 : q * 56 + 56]
        return 0

    lax.fori_loop(0, 4, b_step, 0)
    k1 = scatter("zh", bp, bz)
    w3 = wring.end()
    arrived(w3)

    def w_step(n, _):
        i, j = n // 4, n % 4
        hi, lo = split(jnp.concatenate([wall[i, j, 0], wall[i, j, 1]], axis=1))
        wcat[n, :128] = hi
        wcat[n, 128:256] = lo
        wcat[n, 256:] = hi
        return 0

    lax.fori_loop(0, 16, w_step, 0)
    arrived(og2)
    arrived(k1)
    khi, klo = split(summed(bp[zh], bz).reshape(224, 128))
    kcat = jnp.concatenate([khi, khi, klo], axis=1)

    def f_step(n, _):
        i, j = n // 4, n % 4
        m = mm(kcat, wcat[n])
        half = j // 2
        v = jnp.zeros((56, 256), F32)
        for n_x in range(4):
            v = v + m[n_x * 56 : n_x * 56 + 56] * ogAB[half, i + half * (n_x - i), n_x + half * (i - n_x), j % 2]
        f0[i, j] = jnp.sum(v.reshape(7, 8, 256), axis=0)
        return 0

    lax.fori_loop(0, 16, f_step, 0)
    row = lax.broadcasted_iota(jnp.int32, (8, 256), 0)
    for i in range(4):
        line = jnp.zeros((8, 256), F32)
        for j in range(4):
            line = jnp.where(row == j, jnp.sum(f0[i, j], axis=0, keepdims=True), line)
        f1[i] = line
    got = []
    for n, partner in enumerate(plane):
        i, j = (n + 1) // 4, (n + 1) % 4
        got += start([remote(f1.at[at_distance(c, "y", j)], f2.at[x, y], partner)])
    f2[x, y] = f1[y]
    arrived(got)
    total = jnp.sum(f2[...].reshape(16, 8, 256), axis=0)
    for j in range(4):
        f3[j] = total[j : j + 1]
    got = []
    for n, partner in enumerate(column):
        i, j = (n + 1) // 4, (n + 1) % 4
        got += start([remote(f3.at[at_distance(c, "zh", j)], f4.at[k, zl, zh], partner)])
    f4[k, zl, zh] = f3[zh]
    arrived(got)
    f5[k] = jnp.sum(f4[k].reshape(16, 1, 256), axis=0)
    arrived(start([remote(f5.at[k], f5.at[k], peer(c, "k", 1))]))
    out[...] = f5[0] + f5[1]
    for q in sent:
        q.wait_send()


def body(query_grad, basis_in, basis_out, spectrum, activations, out_grads):
    def vmem(*shape, dtype=F32):
        return pltpu.VMEM(shape, dtype)

    out = pl.pallas_call(
        kernel,
        out_shape=jax.ShapeDtypeStruct((1, 256), F32),
        in_specs=[pl.BlockSpec(memory_space=pl.ANY)] * 6,
        out_specs=pl.BlockSpec(memory_space=pltpu.VMEM),
        scratch_shapes=[
            vmem(4, 4, 112, 448),
            vmem(4, 4, 112, 448),
            vmem(4, 4, 224, 448, dtype=BF16),
            vmem(4, 4, 224, 448, dtype=BF16),
            vmem(4, 224, 128),
            vmem(4, 224, 128),
            vmem(2, 64, 448),
            vmem(2, 224, 128),
            vmem(4, 4, 2, 64, 128),
            vmem(256, 2048, dtype=BF16),
            vmem(2, 4, 4, 64, 128),
            vmem(4, 4, 2, 128, 128),
            vmem(16, 384, 256, dtype=BF16),
            vmem(2, 4, 4, 2, 56, 256),
            vmem(2, 4, 224, 128),
            vmem(4, 224, 128),
            vmem(4, 224, 128),
            vmem(4, 224, 128),
            vmem(4, 4, 112, 128),
            vmem(4, 4, 112, 128),
            vmem(4, 2, 224, 128),
            vmem(4, 448, 256, dtype=BF16),
            vmem(4, 4, 56, 128),
            vmem(4, 4, 56, 128),
            vmem(4, 4, 8, 256),
            vmem(4, 8, 256),
            vmem(4, 4, 8, 256),
            vmem(4, 1, 256),
            vmem(2, 4, 4, 1, 256),
            vmem(2, 1, 256),
            pltpu.SemaphoreType.DMA((N_SEMS,)),
            pltpu.SemaphoreType.DMA((N_SEMS,)),
            pltpu.SemaphoreType.DMA((N_SEMS,)),
        ],
        compiler_params=pltpu.CompilerParams(
            collective_id=0, has_side_effects=True, vmem_limit_bytes=56 * 1024 * 1024
        ),
    )(query_grad, basis_in.T, basis_out, spectrum.T, activations.T, out_grads.T)
    return out.reshape(256)


def solution(mesh):
    in_specs = (
        P("eig", "tok"),
        P("tok", "eig"),
        P("eig", "tok"),
        P("tok", "eig"),
        P("tok", "eig"),
        P("tok", "eig"),
    )
    out_specs = P("tok")
    return jax.shard_map(body, mesh=mesh, in_specs=in_specs, out_specs=out_specs, check_vma=False)
```
